32 devices in a mesh: groups: 2 (over x), leaf: 16 (over z, y, core).
Axes of the slice: x: 2, y: 2, z: 4, core: 2. Of those that a mesh axis runs over, the one named last changes fastest.
Arguments:
- points: float32 [3, 131072], P(None, ('groups', 'leaf')), parts along dimension 1, may hold values from 0 to 1.6, as said below
- input_vectors: float32 [64, 131072], P(None, ('groups', 'leaf')), parts along dimension 1, may hold values from -6 to 6
- leaf_basis: float32 [512, 64, 256], P(('groups', 'leaf')), parts along dimension 0, may hold values from -0.375 to 0.375
- transfer_one: float32 [256, 64, 128], P(('groups', 'leaf')), parts along dimension 0, may hold values from -0.5 to 0.5
- transfer_two: float32 [128, 64, 128], P(('groups', 'leaf')), parts along dimension 0, may hold values from -0.5 to 0.5
- coupling_zero: float32 [512, 64, 512], P(('groups', 'leaf')), parts along dimension 0, may hold values from -0.25 to 0.25
- coupling_one: float32 [256, 64, 512], P(('groups', 'leaf')), parts along dimension 0, may hold values from -0.25 to 0.25
- coupling_two: float32 [128, 64, 512], P(('groups', 'leaf')), parts along dimension 0, may hold values from -0.25 to 0.25
- neighbour_leaves: int32 [512, 16], P(('groups', 'leaf')), parts along dimension 0, may hold values from 0 to 255, as said below
- far_zero: int32 [512, 8], P(('groups', 'leaf')), parts along dimension 0, may hold values from 0 to 255, as said below
- far_one: int32 [256, 8], P(('groups', 'leaf')), parts along dimension 0, may hold values from 0 to 127, as said below
- far_two: int32 [128, 8], P(('groups', 'leaf')), parts along dimension 0, may hold values from 0 to 63, as said below
Outputs:
- kernel_product: float32 [64, 131072], P(None, ('groups', 'leaf')), parts along dimension 1
The draws below stay inside these ranges and needn't reach their ends.
There are 2 independent parts, one for each index of `groups`. The reference program is written for one: setup_inputs(seed, part) draws one part's arguments, and reference() takes and returns one part's arrays. A program takes and returns all parts, laid end to end along the dimension named above; each array names one. Nothing has to cross between parts.
Inputs may be any that keep to these rules, and one draw needn't show every extreme that they name: Each leaf's points lie in a box of side 0.1 of its own; the leaves of one device block of 16 leaves fill one layer of boxes along the third coordinate, in block order. `neighbour_leaves`: entry 0 of a leaf's row is the leaf itself; the others are leaves of the same device block of 16 leaves or of the block just before or after it, and may repeat. `far_zero`: Level-0 nodes are held in blocks of 16; the rows of one block name at most 16 entries, counted with repetition, of any single block, and every block's rows reach that bound for some block. No leaf names itself. `far_one`: Level-1 nodes are held in blocks of 8; the rows of one block name at most 8 entries of any single block, reached by every block's rows. No node names itself. `far_two`: Level-2 nodes are held in blocks of 4; the rows of one block name at most 4 entries of any single block, reached by every block's rows. No node names itself.
All inputs are finite; a program needn't handle non-finite values.
Results may differ from the reference program's by a relative error of at most 0.0003.
Values sent between devices are 32-bit elements; how exact they have to be, the bound alone decides.
No kernel may reach another device: no remote copies, remote signals or barrier semaphores. Data moves between devices by JAX's collectives and lax.ppermute only.
A program may use at most 128 MiB of HBM per device.

```python
import math
import jax
import jax.numpy as jnp
from jax import lax

LEAF = 256
RANK = 64
NRHS = 64
NEAR = 16
FAR = 8
LEAVES_DEV = 16
NLEAF = 256
NPTS = 65536


def far_lists(key, node_count):
    devices = NLEAF // LEAVES_DEV
    entries = node_count * FAR
    mean_count = entries // devices
    keys = jax.random.split(key, 4)
    busiest = jax.random.randint(keys[0], (devices,), 0, devices)
    emptied = (busiest + 1 + jax.random.randint(keys[1], (devices,), 0, devices - 1)) % devices
    holders = jnp.arange(devices, dtype=jnp.int32)
    counts = mean_count + mean_count * (holders[None, :] == busiest[:, None]).astype(jnp.int32) - mean_count * (holders[None, :] == emptied[:, None]).astype(jnp.int32)
    bounds = jnp.cumsum(counts, axis=1)
    position = jnp.arange(entries, dtype=jnp.int32)
    ordered = jnp.sum((position[None, :, None] >= bounds[:, None, :]).astype(jnp.int32), axis=2)
    scores = jax.random.randint(keys[2], (devices, entries), 0, 1 << 16) * entries + position[None, :]
    order = jnp.argsort(scores, axis=1)
    holder = jnp.take_along_axis(ordered, order, axis=1)
    within = jax.random.randint(keys[3], (devices, entries), 0, node_count)
    mine = position // FAR
    same = (holder == holders[:, None]) & (within == mine[None, :])
    within = jnp.where(same, (within + 1) % node_count, within)
    return (holder * node_count + within).reshape(devices * node_count, FAR).astype(jnp.int32)


def draw_points(key, part):
    key = jax.random.fold_in(key, 5)
    leaf_ids = jnp.arange(NLEAF, dtype=jnp.int32)
    slab = leaf_ids // LEAVES_DEV
    inside = leaf_ids % LEAVES_DEV
    corner = jnp.stack([inside % 4, inside // 4, slab]).astype(jnp.float32)
    keys = jax.random.split(key, 2)
    signs = jax.random.normal(keys[0], (3, NLEAF, LEAF), jnp.float32)
    spread = jax.random.uniform(keys[1], (3, NLEAF, LEAF), jnp.float32)
    offsets = 0.5 + 0.4999 * jnp.sign(signs) * (1.0 - spread ** 8)
    return ((corner[:, :, None] + offsets) * 0.1).reshape(3, NPTS).astype(jnp.float32)


def draw_neighbour_leaves(key, part):
    key = jax.random.fold_in(key, 7)
    devices = NLEAF // LEAVES_DEV
    rows_y = LEAVES_DEV // 4
    leaf_ids = jnp.arange(NLEAF, dtype=jnp.int32)
    slab = leaf_ids // LEAVES_DEV
    inside = leaf_ids % LEAVES_DEV
    place_x = inside % 4
    place_y = inside // 4
    steps = jax.random.randint(key, (3, NLEAF, NEAR - 1), -1, 2)
    new_x = jnp.clip(place_x[:, None] + steps[0], 0, 3)
    new_y = jnp.clip(place_y[:, None] + steps[1], 0, rows_y - 1)
    new_z = jnp.clip(slab[:, None] + steps[2], 0, devices - 1)
    others = new_z * LEAVES_DEV + new_y * 4 + new_x
    return jnp.concatenate([leaf_ids[:, None], others], axis=1).astype(jnp.int32)


def draw_far_zero(key, part):
    key = jax.random.fold_in(key, 11)
    return far_lists(key, LEAVES_DEV)


def draw_far_one(key, part):
    key = jax.random.fold_in(key, 12)
    return far_lists(key, LEAVES_DEV // 2)


def draw_far_two(key, part):
    key = jax.random.fold_in(key, 13)
    return far_lists(key, LEAVES_DEV // 4)


def level_of(stream_key, shape, pieces, smallest, largest):
    level, own = 1.0, jax.random.fold_in(stream_key, 6)
    for axis_at, shards_of in pieces:
        steps = jnp.exp(jax.random.uniform(jax.random.fold_in(own, axis_at), (shards_of,), jnp.float32, smallest / len(pieces), largest / len(pieces)))
        level = level * jnp.repeat(steps, shape[axis_at] // shards_of).reshape([-1 if axis == axis_at else 1 for axis in range(len(shape))])
    return level


def noise(own_key, dims, width, limit, cuts=(), held_as=jnp.bfloat16):
    drawn = width * jax.random.normal(own_key, dims, jnp.float32)
    if cuts:
        drawn = drawn * level_of(own_key, dims, cuts, -0.22, 0.18)
    return jnp.clip(drawn, -limit, limit).astype(held_as)


def setup_inputs(seed: int = 0, part: int = 0) -> dict:
    arg_keys = jax.random.split(jax.random.key(seed), 13)
    part_splits = jax.random.split(jax.random.fold_in(arg_keys[12], part), 13)
    points = draw_points(jax.random.fold_in(jax.random.fold_in(arg_keys[12], part), 71), part)
    input_vectors = noise(part_splits[1], (NRHS, NPTS), 1.0, 6.0, ((1, 16),), jnp.float32)
    leaf_basis = noise(part_splits[2], (NLEAF, RANK, LEAF), LEAF ** -0.5, 0.375, ((0, 16),), jnp.float32)
    transfer_one = noise(part_splits[3], (NLEAF // 2, RANK, 2 * RANK), (2 * RANK) ** -0.5, 0.5, ((0, 16),), jnp.float32)
    transfer_two = noise(part_splits[4], (NLEAF // 4, RANK, 2 * RANK), (2 * RANK) ** -0.5, 0.5, ((0, 16),), jnp.float32)
    coupling_zero = noise(part_splits[5], (NLEAF, RANK, FAR * RANK), (FAR * RANK) ** -0.5, 0.25, ((0, 16),), jnp.float32)
    coupling_one = noise(part_splits[6], (NLEAF // 2, RANK, FAR * RANK), (FAR * RANK) ** -0.5, 0.25, ((0, 16),), jnp.float32)
    coupling_two = noise(part_splits[7], (NLEAF // 4, RANK, FAR * RANK), (FAR * RANK) ** -0.5, 0.25, ((0, 16),), jnp.float32)
    neighbour_leaves = draw_neighbour_leaves(jax.random.fold_in(jax.random.fold_in(arg_keys[12], part), 71), part)
    far_zero = draw_far_zero(jax.random.fold_in(jax.random.fold_in(arg_keys[12], part), 71), part)
    far_one = draw_far_one(jax.random.fold_in(jax.random.fold_in(arg_keys[12], part), 71), part)
    far_two = draw_far_two(jax.random.fold_in(jax.random.fold_in(arg_keys[12], part), 71), part)
    return dict(points=points, input_vectors=input_vectors, leaf_basis=leaf_basis, transfer_one=transfer_one, transfer_two=transfer_two, coupling_zero=coupling_zero, coupling_one=coupling_one, coupling_two=coupling_two, neighbour_leaves=neighbour_leaves, far_zero=far_zero, far_one=far_one, far_two=far_two)


highest = lax.Precision.HIGHEST
inverse_scale = math.sqrt(3.0) / 0.05

def matern(squared):
    distance = jnp.sqrt(jnp.maximum(squared, 0.0)) * inverse_scale
    return (1.0 + distance) * jnp.exp(-distance)

def block_contributions(accumulator, evaluation_points, partner_indices):
    source_points = accumulator[:, partner_indices]
    squared = (source_points[0][:, :, :, None] - evaluation_points[0][:, None, None, :]) ** 2
    squared = squared + (source_points[1][:, :, :, None] - evaluation_points[1][:, None, None, :]) ** 2
    squared = squared + (source_points[2][:, :, :, None] - evaluation_points[2][:, None, None, :]) ** 2
    kernel = matern(squared)
    return jnp.einsum('nbks,bkst->nbt', source_points[3:], kernel, precision=highest)

def nearby_interaction(accumulator, points, partner_indices):
    leaf_clusters = partner_indices.shape[0]
    points_per_leaf = points.shape[1] // leaf_clusters
    blocks = leaf_clusters // 2
    targets = jnp.transpose(points.reshape(3, blocks, 2, points_per_leaf), (1, 0, 2, 3))
    partners = partner_indices.reshape(blocks, 2, -1)

    def one_block(element):
        return block_contributions(accumulator, element[0], element[1])
    output_blocks = lax.map(one_block, (targets, partners))
    return jnp.transpose(output_blocks, (1, 0, 2, 3)).reshape(accumulator.shape[0] - 3, -1)

def couple(coupling, coeffs, partners):
    node_count = partners.shape[0]
    flattened = coeffs.reshape(coeffs.shape[0], -1)
    picked = jnp.take(flattened, partners.reshape(-1), axis=0)
    stacked = picked.reshape(node_count, -1, coeffs.shape[2])
    return jnp.einsum('trj,tjn->trn', coupling, stacked, precision=highest)

def reference(points, input_vectors, leaf_basis, transfer_one, transfer_two, coupling_zero, coupling_one, coupling_two, neighbour_leaves, far_zero, far_one, far_two):
    leaf_clusters = leaf_basis.shape[0]
    rank_size = leaf_basis.shape[1]
    rhs_count = input_vectors.shape[0]
    columns = input_vectors.reshape(rhs_count, leaf_clusters, -1)
    coeff_zero = jnp.einsum('lrs,nls->lrn', leaf_basis, columns, precision=highest)
    coeff_one = jnp.einsum('prc,pcn->prn', transfer_one, coeff_zero.reshape(leaf_clusters // 2, 2 * rank_size, rhs_count), precision=highest)
    coeff_two = jnp.einsum('prc,pcn->prn', transfer_two, coeff_one.reshape(leaf_clusters // 4, 2 * rank_size, rhs_count), precision=highest)
    field_zero = couple(coupling_zero, coeff_zero, far_zero)
    field_one = couple(coupling_one, coeff_one, far_one)
    field_two = couple(coupling_two, coeff_two, far_two)
    down_one = field_one + jnp.einsum('prc,prn->pcn', transfer_two, field_two, precision=highest).reshape(leaf_clusters // 2, rank_size, rhs_count)
    down_zero = field_zero + jnp.einsum('prc,prn->pcn', transfer_one, down_one, precision=highest).reshape(leaf_clusters, rank_size, rhs_count)
    far_part = jnp.einsum('lrn,lrs->nls', down_zero, leaf_basis, precision=highest).reshape(rhs_count, -1)
    accumulator = jnp.concatenate([points, input_vectors], axis=0)
    points_per_leaf = points.shape[1] // leaf_clusters
    accumulator = accumulator.reshape(accumulator.shape[0], leaf_clusters, points_per_leaf)
    nearby_portion = nearby_interaction(accumulator, points, neighbour_leaves)
    return nearby_portion + far_part
```

```python
import functools
import math

import jax
import jax.numpy as jnp
from jax import lax
from jax.experimental import pallas as pl
from jax.experimental.pallas import tpu as pltpu
from jax.sharding import PartitionSpec as P

LOG2E = math.log2(math.e)
LN2 = math.log(2.0)
SCALE = math.sqrt(3.0) / 0.05 * LOG2E
TINY = 1e-10
NN = (((1,), (0,)), ((), ()))
NT = (((1,), (1,)), ((), ()))
VMEM_LIMIT = 56 * 1024 * 1024


def halves(value):
    high = value.astype(jnp.bfloat16)
    low = (value - high.astype(jnp.float32)).astype(jnp.bfloat16)
    return high, low


def product(left, right, dims):
    left_high, left_low = halves(left)
    right_high, right_low = halves(right)
    dot = functools.partial(lax.dot_general, preferred_element_type=jnp.float32)
    return (
        dot(left_high, right_high, dims)
        + dot(left_high, right_low, dims)
        + dot(left_low, right_high, dims)
    )


def up_kernel(vectors, basis, first, second, out):
    leaves, _, size = basis.shape
    rank = basis.shape[1]
    pairs = []
    for pair in range(leaves // 2):
        both = []
        for leaf in (2 * pair, 2 * pair + 1):
            columns = vectors[:, leaf * size : (leaf + 1) * size]
            both.append(product(columns, basis[leaf], NT))
        pairs.append(jnp.concatenate(both, axis=1))
        out[pair] = pairs[pair]
    base = len(pairs)
    for transfer in (first, second):
        nodes = [product(pairs[i], transfer[i], NT) for i in range(len(pairs))]
        pairs = [
            jnp.concatenate(nodes[2 * i : 2 * i + 2], axis=1) for i in range(len(nodes) // 2)
        ]
        for i, pair in enumerate(pairs):
            out[base + i] = pair
        base += len(pairs)


def thirds(value):
    high = value.astype(jnp.bfloat16).astype(jnp.float32)
    rest = value - high
    middle = rest.astype(jnp.bfloat16).astype(jnp.float32)
    low = (rest - middle).astype(jnp.bfloat16).astype(jnp.float32)
    return high, middle, low


def features(points, centre, source):
    scaled = (points - centre) * SCALE
    high, middle, low = thirds(scaled)
    square = jnp.sum(scaled * scaled, axis=0, keepdims=True)
    parts = jnp.concatenate(thirds(square), axis=0)
    ones = jnp.ones_like(parts)
    pad = jnp.zeros((8, points.shape[1]), jnp.float32)
    if source:
        rows = [high, high, middle, middle, high, low, parts, ones, pad]
    else:
        rows = [-2.0 * v for v in (high, middle, high, middle, low, high)]
        rows += [ones, parts, pad]
    return jnp.concatenate(rows, axis=0)


def near_kernel(
    partners, v_own, v_before, v_after, p_own, p_before, p_after, out, split, source, target, total
):
    leaves, _, size = target.shape
    count = partners.shape[1]
    rhs = v_own.shape[0]
    own = p_own[...]
    top = jnp.max(own, axis=1, keepdims=True)
    bottom = jnp.min(own, axis=1, keepdims=True)
    centre = 0.5 * (top + bottom)
    wide = features(own, centre, False).astype(jnp.bfloat16)
    for leaf in range(leaves):
        target[leaf] = wide[:, leaf * size : (leaf + 1) * size]
    for block, (vectors, points) in enumerate(
        ((v_before, p_before), (v_own, p_own), (v_after, p_after))
    ):
        wide = features(points[...], centre, True)
        for leaf in range(leaves):
            cut = slice(leaf * size, (leaf + 1) * size)
            at = block * leaves + leaf
            source[at] = wide[:, cut].T.astype(jnp.bfloat16)
            high, low = halves(vectors[:, cut])
            split[at, :rhs] = high
            split[at, rhs:] = low

    def one_target(leaf, carry):
        here = target[leaf]
        total[...] = jnp.zeros_like(total)

        def one_partner(k, carry):
            at = partners[leaf, k]
            square = lax.dot_general(source[at], here, NN, preferred_element_type=jnp.float32)
            square = jnp.maximum(square, TINY)
            distance = square * lax.rsqrt(square)
            value = (distance + LOG2E) * jnp.exp2(-distance)
            high, low = halves(value)
            both = split[at]
            first = lax.dot_general(both, high, NN, preferred_element_type=jnp.float32)
            second = lax.dot_general(both[:rhs], low, NN, preferred_element_type=jnp.float32)
            total[:rhs] += first[:rhs] + second
            total[rhs:] += first[rhs:]
            return carry

        lax.fori_loop(0, count, one_partner, 0)
        start = pl.multiple_of(leaf * size, size)
        out[:, pl.ds(start, size)] = (total[:rhs] + total[rhs:]) * LN2
        return carry

    lax.fori_loop(0, leaves, one_target, 0)


def down_kernel(codes, *refs):
    slots = refs[:-11]
    near, basis, first, second, c_zero, c_one, c_two, out, table, fields, sems = refs[-11:]
    units = slots[0].shape[0]
    copies = []
    for i, slot in enumerate(slots):
        copies.append(
            pltpu.make_async_copy(slot, table.at[pl.ds(i * units, units)], sems.at[i])
        )
    for copy in copies:
        copy.start()
    for copy in copies:
        copy.wait()
    leaves, rank, size = basis.shape
    rhs = near.shape[0]
    lane = lax.broadcasted_iota(jnp.int32, (rhs, 2 * rank), 1)
    partner_count = codes.shape[1]

    def field(node, coupling):
        pieces = []
        for k in range(0, partner_count, 2):
            even, odd = codes[node, k], codes[node, k + 1]
            left = pltpu.roll(table[even // 2], (even % 2) * rank, 1)
            right = pltpu.roll(table[odd // 2], (1 - odd % 2) * rank, 1)
            pieces.append(jnp.where(lane < rank, left, right))
        return product(jnp.concatenate(pieces, axis=1), coupling, NT)

    def level(base, coupling):
        def step(i, carry):
            at = base + i
            even = field(2 * at, coupling[2 * i])
            odd = field(2 * at + 1, coupling[2 * i + 1])
            fields[at] = jnp.concatenate([even, odd], axis=1)
            return carry

        lax.fori_loop(0, coupling.shape[0] // 2, step, 0)

    level(0, c_zero)
    level(leaves // 2, c_one)
    level(leaves // 2 + leaves // 4, c_two)

    ones = []
    for p in range(leaves // 4):
        pair = fields[leaves // 2 + leaves // 4 + p // 2]
        top = pair[:, :rank] if p % 2 == 0 else pair[:, rank:]
        ones.append(fields[leaves // 2 + p] + product(top, second[p], NN))
    for p in range(leaves // 2):
        pair = ones[p // 2]
        top = pair[:, :rank] if p % 2 == 0 else pair[:, rank:]
        zeros = fields[p] + product(top, first[p], NN)
        for half in range(2):
            leaf = 2 * p + half
            low = zeros[:, :rank] if half == 0 else zeros[:, rank:]
            cut = slice(leaf * size, (leaf + 1) * size)
            out[:, cut] = near[:, cut] + product(low, basis[leaf], NN)


def whole_vmem(n):
    return [pl.BlockSpec(memory_space=pltpu.VMEM)] * n


def params():
    return pltpu.CompilerParams(vmem_limit_bytes=VMEM_LIMIT)


def on_device(
    devices,
    points,
    input_vectors,
    leaf_basis,
    transfer_one,
    transfer_two,
    coupling_zero,
    coupling_one,
    coupling_two,
    neighbour_leaves,
    far_zero,
    far_one,
    far_two,
):
    leaves, rank, size = leaf_basis.shape
    rhs = input_vectors.shape[0]
    me = lax.axis_index("leaf")
    up = [(i, i + 1) for i in range(devices - 1)]
    down = [(i + 1, i) for i in range(devices - 1)]
    v_before = lax.ppermute(input_vectors, "leaf", up)
    v_after = lax.ppermute(input_vectors, "leaf", down)
    p_before = lax.ppermute(points, "leaf", up)
    p_after = lax.ppermute(points, "leaf", down)

    units = leaves // 2 + leaves // 4 + leaves // 8
    coeffs = pl.pallas_call(
        up_kernel,
        out_shape=jax.ShapeDtypeStruct((units, rhs, 2 * rank), jnp.float32),
        in_specs=whole_vmem(4),
        out_specs=pl.BlockSpec(memory_space=pltpu.VMEM),
        compiler_params=params(),
        name="up",
    )(input_vectors, leaf_basis, transfer_one, transfer_two)

    lines = devices // 4

    def swap(value, line_step, row_flip, core_flip):
        pairs = []
        for i in range(devices):
            line, row, core = i // 4, i // 2 % 2, i % 2
            there = ((line + line_step) % lines * 2 + (row ^ row_flip)) * 2 + (core ^ core_flip)
            pairs.append((i, there))
        return lax.ppermute(value, "leaf", pairs)

    along = [coeffs] + [swap(coeffs, k, 0, 0) for k in range(1, lines)]
    across = [swap(value, 0, 1, 0) for value in along]
    near_side = along + across
    slots = near_side + [swap(value, 0, 0, 1) for value in near_side]

    first_leaf = (me - 1) * leaves
    near = pl.pallas_call(
        near_kernel,
        out_shape=jax.ShapeDtypeStruct(input_vectors.shape, jnp.float32),
        in_specs=[pl.BlockSpec(memory_space=pltpu.SMEM)] + whole_vmem(6),
        out_specs=pl.BlockSpec(memory_space=pltpu.VMEM),
        scratch_shapes=[
            pltpu.VMEM((3 * leaves, 2 * rhs, size), jnp.bfloat16),
            pltpu.VMEM((3 * leaves, size, 32), jnp.bfloat16),
            pltpu.VMEM((leaves, 32, size), jnp.bfloat16),
            pltpu.VMEM((2 * rhs, size), jnp.float32),
        ],
        compiler_params=params(),
        name="near",
    )(
        neighbour_leaves - first_leaf,
        input_vectors,
        v_before,
        v_after,
        points,
        p_before,
        p_after,
    )

    codes = []
    base = 0
    for partners, nodes in ((far_zero, leaves), (far_one, leaves // 2), (far_two, leaves // 4)):
        owner = partners // nodes
        local = partners % nodes
        step = (me // 4 - owner // 4 + lines) % lines
        row = (me // 2 + owner // 2) % 2
        core = (me + owner) % 2
        slot = (core * 2 + row) * lines + step
        codes.append((slot * units + base + local // 2) * 2 + local % 2)
        base += nodes // 2
    codes = jnp.concatenate(codes, axis=0)

    return pl.pallas_call(
        down_kernel,
        out_shape=jax.ShapeDtypeStruct(input_vectors.shape, jnp.float32),
        in_specs=[pl.BlockSpec(memory_space=pltpu.SMEM)]
        + [pl.BlockSpec(memory_space=pl.ANY)] * len(slots)
        + whole_vmem(7),
        out_specs=pl.BlockSpec(memory_space=pltpu.VMEM),
        scratch_shapes=[
            pltpu.VMEM((len(slots) * units, rhs, 2 * rank), jnp.float32),
            pltpu.VMEM((units, rhs, 2 * rank), jnp.float32),
            pltpu.SemaphoreType.DMA((len(slots),)),
        ],
        compiler_params=params(),
        name="down",
    )(
        codes,
        *slots,
        near,
        leaf_basis,
        transfer_one,
        transfer_two,
        coupling_zero,
        coupling_one,
        coupling_two,
    )


def solution(mesh):
    whole = ("groups", "leaf")
    columns, nodes, lists = P(None, whole), P(whole, None, None), P(whole, None)
    return jax.shard_map(
        functools.partial(on_device, mesh.shape["leaf"]),
        mesh=mesh,
        in_specs=(columns, columns) + (nodes,) * 6 + (lists,) * 4,
        out_specs=columns,
        check_vma=False,
    )
```

```python
import functools
import math

import jax
import jax.numpy as jnp
from jax import lax
from jax.experimental import pallas as pl
from jax.experimental.pallas import tpu as pltpu
from jax.sharding import PartitionSpec as P

LOG2E = math.log2(math.e)
LN2 = math.log(2.0)
SCALE = math.sqrt(3.0) / 0.05 * LOG2E
TINY = 1e-10
NN = (((1,), (0,)), ((), ()))
NT = (((1,), (1,)), ((), ()))
GROUP = 8
NEAR_WORK = 10**10
OWN_WORK = 10**6
DOWN_MEBIBYTES = 56


def halves(value):
    high = value.astype(jnp.bfloat16)
    low = (value - high.astype(jnp.float32)).astype(jnp.bfloat16)
    return high, low


def product(left, right, dims):
    left_high, left_low = halves(left)
    right_high, right_low = halves(right)
    dot = functools.partial(lax.dot_general, preferred_element_type=jnp.float32)
    return (
        dot(left_high, right_high, dims)
        + dot(left_high, right_low, dims)
        + dot(left_low, right_high, dims)
    )


def up_kernel(neighbours, vectors, basis, first, second, _, out, lists):
    me = lax.axis_index("leaf")
    leaves, _, size = basis.shape
    rank = basis.shape[1]
    pairs = []
    for pair in range(leaves // 2):
        both = []
        for leaf in (2 * pair, 2 * pair + 1):
            columns = vectors[:, leaf * size : (leaf + 1) * size]
            both.append(product(columns, basis[leaf], NT))
        pairs.append(jnp.concatenate(both, axis=1))
        out[pair] = pairs[pair]
    base = len(pairs)
    for transfer in (first, second):
        nodes = [product(pairs[i], transfer[i], NT) for i in range(len(pairs))]
        pairs = [
            jnp.concatenate(nodes[2 * i : 2 * i + 2], axis=1) for i in range(len(nodes) // 2)
        ]
        for i, pair in enumerate(pairs):
            out[base + i] = pair
        base += len(pairs)
    pair_lists(neighbours[...] - (me - 1) * leaves, leaves, lists)


def pick_kernel(lines, leaves, units, far_zero, far_one, far_two, codes):
    me = lax.axis_index("leaf")
    unit, row = 0, 0
    for far, nodes in ((far_zero, leaves), (far_one, leaves // 2), (far_two, leaves // 4)):
        owner = far[...] // nodes
        local = far[...] % nodes
        step = (me // 4 - owner // 4 + lines) % lines
        across = (me // 2 + owner // 2) % 2
        core = (me + owner) % 2
        slot = (core * 2 + across) * lines + step
        codes[row : row + nodes] = (slot * units + unit + local // 2) * 2 + local % 2
        unit += nodes // 2
        row += nodes


def thirds(value):
    high = value.astype(jnp.bfloat16).astype(jnp.float32)
    rest = value - high
    middle = rest.astype(jnp.bfloat16).astype(jnp.float32)
    low = (rest - middle).astype(jnp.bfloat16).astype(jnp.float32)
    return high, middle, low


def features(points, centre, source):
    scaled = (points - centre) * SCALE
    high, middle, low = thirds(scaled)
    square = jnp.sum(scaled * scaled, axis=0, keepdims=True)
    parts = jnp.concatenate(thirds(square), axis=0)
    ones = jnp.ones_like(parts)
    pad = jnp.zeros((8, points.shape[1]), jnp.float32)
    if source:
        rows = [high, high, middle, middle, high, low, parts, ones, pad]
    else:
        rows = [-2.0 * v for v in (high, middle, high, middle, low, high)]
        rows += [ones, parts, pad]
    return jnp.concatenate(rows, axis=0)


def pair_lists(relative, leaves, out):
    targets, count = relative.shape
    ids = relative.astype(jnp.float32)
    column = lax.broadcasted_iota(jnp.int32, (targets, count), 1)
    row = lax.broadcasted_iota(jnp.int32, (targets, count), 0)
    times = jnp.zeros((targets, count), jnp.float32)
    earlier = jnp.zeros((targets, count), jnp.float32)
    for k in range(count):
        same = jnp.where(ids == ids[:, k : k + 1], 1.0, 0.0)
        times += same
        earlier += jnp.where(column > k, same, 0.0)
    before = jnp.where(
        lax.broadcasted_iota(jnp.int32, (count, count), 0)
        < lax.broadcasted_iota(jnp.int32, (count, count), 1),
        1.0,
        0.0,
    )
    above = jnp.where(
        lax.broadcasted_iota(jnp.int32, (targets, targets), 1)
        < lax.broadcasted_iota(jnp.int32, (targets, targets), 0),
        1.0,
        0.0,
    )
    width = targets * count
    place = lax.broadcasted_iota(jnp.int32, (targets, width), 1).astype(jnp.float32)
    for i in range(3):
        source = relative - i * leaves
        keep = jnp.where((source >= 0) & (source < leaves) & (earlier == 0.0), 1.0, 0.0)
        rank = lax.dot_general(keep, before, NN, preferred_element_type=jnp.float32)
        sums = jnp.sum(keep, axis=1, keepdims=True)
        wide = jnp.broadcast_to(sums, (targets, count))
        rank += lax.dot_general(above, wide, NN, preferred_element_type=jnp.float32)
        code = (times * targets + row.astype(jnp.float32)) * leaves
        code = (code + source.astype(jnp.float32)) * keep
        rank = jnp.where(keep > 0.0, rank, -1.0)
        flat = jnp.zeros((targets, width), jnp.float32)
        for k in range(count):
            flat += jnp.where(rank[:, k : k + 1] == place, code[:, k : k + 1], 0.0)
        out[i : i + 1] = jnp.sum(flat, axis=0, keepdims=True).astype(jnp.int32)
        total = jnp.sum(sums, axis=0, keepdims=True)
        out[i + 3 : i + 4] = jnp.broadcast_to(total, (1, width)).astype(jnp.int32)


def near_kernel(which, leaves, lists, p_own, block, *refs):
    so_far = None if which == 1 else refs[0]
    out, split, source, target, total = refs[-5:]
    rhs, size = split.shape[1] // 2, split.shape[2]
    own = p_own[...]
    top = jnp.max(own, axis=1, keepdims=True)
    bottom = jnp.min(own, axis=1, keepdims=True)
    centre = 0.5 * (top + bottom)
    wide = features(own, centre, False).astype(jnp.bfloat16)
    there = features(block[rhs : rhs + 3], centre, True)
    for leaf in range(leaves):
        cut = slice(leaf * size, (leaf + 1) * size)
        target[leaf] = wide[:, cut]
        total[leaf] = jnp.zeros(total.shape[1:], jnp.float32)
        source[leaf] = there[:, cut].T.astype(jnp.bfloat16)
        high, low = halves(block[:rhs, cut])
        split[leaf, :rhs] = high
        split[leaf, rhs:] = low

    dot = functools.partial(lax.dot_general, preferred_element_type=jnp.float32)

    def group(step, carry):
        for i in range(GROUP):
            code = lists[which, step * GROUP + i]
            at = code % leaves
            rest = code // leaves
            into = rest % leaves
            times = (rest // leaves).astype(jnp.float32)
            square = jnp.maximum(dot(source[at], target[into], NN), TINY)
            distance = square * lax.rsqrt(square)
            high, low = halves((distance + LOG2E) * jnp.exp2(-distance))
            both = split[at]
            total[into] += (dot(both, high, NN) + dot(both, low, NN)) * times
        return carry

    lax.fori_loop(0, (lists[which + 3, 0] + GROUP - 1) // GROUP, group, 0)
    for leaf in range(leaves):
        cut = slice(leaf * size, (leaf + 1) * size)
        value = (total[leaf, :rhs] + total[leaf, rhs:]) * LN2
        out[:, cut] = value if so_far is None else so_far[:, cut] + value


def down_kernel(codes, *refs):
    slots = refs[:-17]
    sources, out = refs[-17:-10], refs[-10]
    table, fields, *held, sems = refs[-9:]
    second, c_two, c_one, c_zero, first, basis = held
    units = slots[0].shape[0]
    targets = [table.at[pl.ds(i * units, units)] for i in range(len(slots))]
    targets += held + [out]
    copies = [
        pltpu.make_async_copy(source, target, sems.at[i])
        for i, (source, target) in enumerate(zip(slots + sources, targets))
    ]
    for copy in copies:
        copy.start()
    for copy in copies[: len(slots) + 2]:
        copy.wait()
    leaves, rank, size = basis.shape
    rhs = out.shape[0]
    lane = lax.broadcasted_iota(jnp.int32, (rhs, 2 * rank), 1)
    partner_count = codes.shape[1]

    def field(node, coupling):
        pieces = []
        for k in range(0, partner_count, 2):
            even, odd = codes[node, k], codes[node, k + 1]
            left = pltpu.roll(table[even // 2], (even % 2) * rank, 1)
            right = pltpu.roll(table[odd // 2], (1 - odd % 2) * rank, 1)
            pieces.append(jnp.where(lane < rank, left, right))
        return product(jnp.concatenate(pieces, axis=1), coupling, NT)

    def level(base, coupling):
        def step(i, carry):
            for j in range(2):
                at = 2 * i + j
                even = field(2 * (base + at), coupling[2 * at])
                odd = field(2 * (base + at) + 1, coupling[2 * at + 1])
                fields[base + at] = jnp.concatenate([even, odd], axis=1)
            return carry

        lax.fori_loop(0, coupling.shape[0] // 4, step, 0)

    level(leaves // 2 + leaves // 4, c_two)
    copies[len(slots) + 2].wait()
    level(leaves // 2, c_one)
    copies[len(slots) + 3].wait()
    level(0, c_zero)
    for copy in copies[len(slots) + 4 :]:
        copy.wait()

    ones = []
    for p in range(leaves // 4):
        pair = fields[leaves // 2 + leaves // 4 + p // 2]
        top = pair[:, :rank] if p % 2 == 0 else pair[:, rank:]
        ones.append(fields[leaves // 2 + p] + product(top, second[p], NN))
    for p in range(leaves // 2):
        pair = ones[p // 2]
        top = pair[:, :rank] if p % 2 == 0 else pair[:, rank:]
        zeros = fields[p] + product(top, first[p], NN)
        for half in range(2):
            leaf = 2 * p + half
            low = zeros[:, :rank] if half == 0 else zeros[:, rank:]
            cut = slice(leaf * size, (leaf + 1) * size)
            out[:, cut] += product(low, basis[leaf], NN)


def whole_vmem(n):
    return [pl.BlockSpec(memory_space=pltpu.VMEM)] * n


def params(mebibytes):
    return pltpu.CompilerParams(vmem_limit_bytes=mebibytes * 2**20)


def on_device(
    devices,
    points,
    input_vectors,
    leaf_basis,
    transfer_one,
    transfer_two,
    coupling_zero,
    coupling_one,
    coupling_two,
    neighbour_leaves,
    far_zero,
    far_one,
    far_two,
):
    leaves, rank, size = leaf_basis.shape
    rhs = input_vectors.shape[0]
    tie = lax.optimization_barrier
    before = [(i, i + 1) for i in range(devices - 1)]
    after = [(i + 1, i) for i in range(devices - 1)]
    stacked = jnp.concatenate([input_vectors, points], axis=0)
    from_before = lax.ppermute(stacked, "leaf", before)
    from_after = lax.ppermute(stacked, "leaf", after)

    lines = devices // 4

    def swap(value, line_step, row_flip, core_flip):
        pairs = []
        for i in range(devices):
            line, row, core = i // 4, i // 2 % 2, i % 2
            there = ((line + line_step) % lines * 2 + (row ^ row_flip)) * 2 + (core ^ core_flip)
            pairs.append((i, there))
        return lax.ppermute(value, "leaf", pairs)

    units = leaves // 2 + leaves // 4 + leaves // 8
    nodes = leaves + leaves // 2 + leaves // 4
    near_count, far_count = neighbour_leaves.shape[1], far_zero.shape[1]
    coeffs, lists = pl.pallas_call(
        up_kernel,
        out_shape=(
            jax.ShapeDtypeStruct((units, rhs, 2 * rank), jnp.float32),
            jax.ShapeDtypeStruct((6, leaves * near_count), jnp.int32),
        ),
        in_specs=whole_vmem(5) + [pl.BlockSpec(memory_space=pl.ANY)],
        out_specs=tuple(whole_vmem(2)),
        compiler_params=params(12),
        name="up",
    )(neighbour_leaves, input_vectors, leaf_basis, transfer_one, transfer_two, stacked)
    codes = pl.pallas_call(
        functools.partial(pick_kernel, lines, leaves, units),
        out_shape=jax.ShapeDtypeStruct((nodes, far_count), jnp.int32),
        in_specs=whole_vmem(3),
        out_specs=pl.BlockSpec(memory_space=pltpu.VMEM),
        compiler_params=params(2),
        name="picks",
    )(far_zero, far_one, far_two)

    def near_field(which, operand, work, near, *later):
        operands = (operand,) if near is None else (operand, near)
        return pl.pallas_call(
            functools.partial(near_kernel, which, leaves),
            out_shape=jax.ShapeDtypeStruct(input_vectors.shape, jnp.float32),
            in_specs=[pl.BlockSpec(memory_space=pltpu.SMEM)]
            + whole_vmem(1 + len(operands))
            + [pl.BlockSpec(memory_space=pl.ANY)] * len(later),
            out_specs=pl.BlockSpec(memory_space=pltpu.VMEM),
            scratch_shapes=[
                pltpu.VMEM((leaves, 2 * rhs, size), jnp.bfloat16),
                pltpu.VMEM((leaves, size, 32), jnp.bfloat16),
                pltpu.VMEM((leaves, 32, size), jnp.bfloat16),
                pltpu.VMEM((leaves, 2 * rhs, size), jnp.float32),
            ],
            cost_estimate=pl.CostEstimate(
                flops=work, bytes_accessed=3 * 2**20, transcendentals=0
            ),
            compiler_params=params(16),
            name=("near_before", "near_own", "near_after")[which],
        )(lists, points, *operands, *later)

    far_end = lines - 1
    held = {(0, 0): coeffs}
    for step, towards in {1: 1, far_end: -1}.items():
        held[0, step] = swap(coeffs, towards, 0, 0)
    held[1, 0] = swap(coeffs, 0, 1, 0)
    near = near_field(1, stacked, OWN_WORK, None)
    held, near = tie((held, near))
    middle = (lines + 1) // 2
    for step in range(2, middle + 1):
        if (0, step) not in held:
            held[0, step] = swap(held[0, step - 1], 1, 0, 0)
    for step in range(far_end - 1, middle, -1):
        held[0, step] = swap(held[0, step + 1], -1, 0, 0)
    if far_end > 1:
        held[1, far_end] = swap(held[0, far_end], 0, 1, 0)
    ends = [held[0, step] for step in sorted({1, far_end})]
    near = near_field(0, from_before, NEAR_WORK, near, from_after, *ends)
    along, near = tie(([held[0, step] for step in range(lines)], near))
    if (1, 1) not in held:
        behind, _ = tie((held[1, 0], along))
        held[1, 1] = swap(behind, 1, 0, 0)
    for step in range(2, far_end):
        held[1, step] = swap(along[step], 0, 1, 0)
    early = {(0, step): value for step, value in enumerate(along)}
    early[1, 0], near = tie((held[1, 0], near))
    across = {key: swap(value, 0, 0, 1) for key, value in early.items()}
    near = near_field(2, from_after, NEAR_WORK, near, *along[2:far_end])
    late = {key: value for key, value in held.items() if key not in early}
    late, near = tie((late, near))
    across.update({key: swap(value, 0, 0, 1) for key, value in late.items()})
    order = [(row, step) for row in range(2) for step in range(lines)]
    slots = [{**early, **late}[key] for key in order] + [across[key] for key in order]

    operands = (
        transfer_two,
        coupling_two,
        coupling_one,
        coupling_zero,
        transfer_one,
        leaf_basis,
    )
    copied = len(slots) + len(operands) + 1
    return pl.pallas_call(
        down_kernel,
        out_shape=jax.ShapeDtypeStruct(input_vectors.shape, jnp.float32),
        in_specs=[pl.BlockSpec(memory_space=pltpu.SMEM)]
        + [pl.BlockSpec(memory_space=pl.ANY)] * copied,
        out_specs=pl.BlockSpec(memory_space=pltpu.VMEM),
        scratch_shapes=[
            pltpu.VMEM((devices * units, rhs, 2 * rank), jnp.float32),
            pltpu.VMEM((units, rhs, 2 * rank), jnp.float32),
        ]
        + [pltpu.VMEM(operand.shape, jnp.float32) for operand in operands]
        + [pltpu.SemaphoreType.DMA((copied,))],
        compiler_params=params(DOWN_MEBIBYTES),
        name="down",
    )(codes, *slots, *operands, near)


def solution(mesh):
    whole = ("groups", "leaf")
    columns, nodes, lists = P(None, whole), P(whole, None, None), P(whole, None)
    return jax.shard_map(
        functools.partial(on_device, mesh.shape["leaf"]),
        mesh=mesh,
        in_specs=(columns, columns) + (nodes,) * 6 + (lists,) * 4,
        out_specs=columns,
        check_vma=False,
    )
```

```python
import functools
import math

import jax
import jax.numpy as jnp
from jax import lax
from jax.experimental import pallas as pl
from jax.experimental.pallas import tpu as pltpu
from jax.sharding import PartitionSpec as P

LOG2E = math.log2(math.e)
LN2 = math.log(2.0)
SCALE = math.sqrt(3.0) / 0.05 * LOG2E
TINY = 1e-10
NN = (((1,), (0,)), ((), ()))
NT = (((1,), (1,)), ((), ()))
GROUP = 8
NEAR_WORK = 10**10
OWN_WORK = 10**6
NEAR_MEBIBYTES = 16
DOWN_MEBIBYTES = 56


def halves(value):
    high = value.astype(jnp.bfloat16)
    low = (value - high.astype(jnp.float32)).astype(jnp.bfloat16)
    return high, low


def product(left, right, dims):
    across = 1 if dims == NN else 0
    both = lax.dot_general(
        jnp.concatenate(halves(left), axis=0),
        jnp.concatenate(halves(right), axis=across),
        dims,
        preferred_element_type=jnp.float32,
    )
    rows = left.shape[0]
    return both[:rows] + both[rows:]


def folded(wide):
    return wide + pltpu.roll(wide, wide.shape[1] // 2, 1)


def narrow(wide):
    width = wide.shape[1] // 2
    return wide[:, :width] + wide[:, width:]


def pair_of(even, odd):
    lane = lax.broadcasted_iota(jnp.int32, even.shape, 1)
    return jnp.where(lane < even.shape[1] // 2, folded(even), folded(odd))


def up_kernel(neighbours, vectors, basis, first, second, _, out, lists):
    me = lax.axis_index("leaf")
    leaves, _, size = basis.shape
    pairs = []
    for pair in range(leaves // 2):
        both = []
        for leaf in (2 * pair, 2 * pair + 1):
            columns = vectors[:, leaf * size : (leaf + 1) * size]
            both.append(product(columns, basis[leaf], NT))
        pairs.append(pair_of(*both))
        out[pair] = pairs[pair]
    base = len(pairs)
    for transfer in (first, second):
        nodes = [product(pairs[i], transfer[i], NT) for i in range(len(pairs))]
        pairs = [pair_of(*nodes[2 * i : 2 * i + 2]) for i in range(len(nodes) // 2)]
        for i, pair in enumerate(pairs):
            out[base + i] = pair
        base += len(pairs)
    pair_lists(neighbours[...] - (me - 1) * leaves, leaves, lists)


def pick_kernel(lines, leaves, units, far_zero, far_one, far_two, codes):
    me = lax.axis_index("leaf")
    unit, row = 0, 0
    for far, nodes in ((far_zero, leaves), (far_one, leaves // 2), (far_two, leaves // 4)):
        owner = far[...] // nodes
        local = far[...] % nodes
        step = (me // 4 - owner // 4 + lines) % lines
        across = (me // 2 + owner // 2) % 2
        core = (me + owner) % 2
        slot = (core * 2 + across) * lines + step
        codes[row : row + nodes] = (slot * units + unit + local // 2) * 2 + local % 2
        unit += nodes // 2
        row += nodes


def thirds(value):
    high = value.astype(jnp.bfloat16).astype(jnp.float32)
    rest = value - high
    middle = rest.astype(jnp.bfloat16).astype(jnp.float32)
    low = (rest - middle).astype(jnp.bfloat16).astype(jnp.float32)
    return high, middle, low


def features(points, centre, source):
    scaled = (points - centre) * SCALE
    high, middle, low = thirds(scaled)
    square = jnp.sum(scaled * scaled, axis=0, keepdims=True)
    parts = jnp.concatenate(thirds(square), axis=0)
    ones = jnp.ones_like(parts)
    pad = jnp.zeros((8, points.shape[1]), jnp.float32)
    if source:
        rows = [high, high, middle, middle, high, low, parts, ones, pad]
    else:
        rows = [-2.0 * v for v in (high, middle, high, middle, low, high)]
        rows += [ones, parts, pad]
    return jnp.concatenate(rows, axis=0)


def pair_lists(relative, leaves, out):
    targets, count = relative.shape
    ids = relative.astype(jnp.float32)
    column = lax.broadcasted_iota(jnp.int32, (targets, count), 1)
    row = lax.broadcasted_iota(jnp.int32, (targets, count), 0)
    times = jnp.zeros((targets, count), jnp.float32)
    earlier = jnp.zeros((targets, count), jnp.float32)
    for k in range(count):
        same = jnp.where(ids == ids[:, k : k + 1], 1.0, 0.0)
        times += same
        earlier += jnp.where(column > k, same, 0.0)
    before = jnp.where(
        lax.broadcasted_iota(jnp.int32, (count, count), 0)
        < lax.broadcasted_iota(jnp.int32, (count, count), 1),
        1.0,
        0.0,
    )
    above = jnp.where(
        lax.broadcasted_iota(jnp.int32, (targets, targets), 1)
        < lax.broadcasted_iota(jnp.int32, (targets, targets), 0),
        1.0,
        0.0,
    )
    width = targets * count
    place = lax.broadcasted_iota(jnp.int32, (targets, width), 1).astype(jnp.float32)
    for i in range(3):
        source = relative - i * leaves
        keep = jnp.where((source >= 0) & (source < leaves) & (earlier == 0.0), 1.0, 0.0)
        rank = lax.dot_general(keep, before, NN, preferred_element_type=jnp.float32)
        sums = jnp.sum(keep, axis=1, keepdims=True)
        wide = jnp.broadcast_to(sums, (targets, count))
        rank += lax.dot_general(above, wide, NN, preferred_element_type=jnp.float32)
        code = (times * targets + row.astype(jnp.float32)) * leaves
        code = (code + source.astype(jnp.float32)) * keep
        rank = jnp.where(keep > 0.0, rank, -1.0)
        flat = jnp.zeros((targets, width), jnp.float32)
        for k in range(count):
            flat += jnp.where(rank[:, k : k + 1] == place, code[:, k : k + 1], 0.0)
        out[i : i + 1] = jnp.sum(flat, axis=0, keepdims=True).astype(jnp.int32)
        total = jnp.sum(sums, axis=0, keepdims=True)
        out[i + 3 : i + 4] = jnp.broadcast_to(total, (1, width)).astype(jnp.int32)


def pack_kernel(vectors, points, out, sem):
    width = vectors.shape[1]
    copy = pltpu.make_async_copy(vectors, out.at[:, pl.ds(0, width)], sem)
    copy.start()
    size = out.shape[1] - width
    out[:, width:] = jnp.zeros((out.shape[0], size), jnp.float32)
    for leaf in range(width // size):
        cut = slice(leaf * size, (leaf + 1) * size)
        out[4 * leaf : 4 * leaf + 3, width:] = points[:, cut]
    copy.wait()


def near_kernel(which, part, leaves, lists, p_own, block, *refs):
    so_far = None if which == 1 else refs[0]
    out, split, source, target, total = refs[-5:]
    rhs, size = split.shape[1] // 2, split.shape[2]
    own = p_own[...]
    top = jnp.max(own, axis=1, keepdims=True)
    bottom = jnp.min(own, axis=1, keepdims=True)
    centre = 0.5 * (top + bottom)
    wide = features(own, centre, False).astype(jnp.bfloat16)
    wide_points = [block[4 * leaf : 4 * leaf + 3, leaves * size :] for leaf in range(leaves)]
    there = features(jnp.concatenate(wide_points, axis=1), centre, True)
    for leaf in range(leaves):
        cut = slice(leaf * size, (leaf + 1) * size)
        target[leaf] = wide[:, cut]
        total[leaf] = jnp.zeros(total.shape[1:], jnp.float32)
        source[leaf] = there[:, cut].T.astype(jnp.bfloat16)
        high, low = halves(block[:rhs, cut])
        split[leaf, :rhs] = high
        split[leaf, rhs:] = low

    dot = functools.partial(lax.dot_general, preferred_element_type=jnp.float32)

    def group(step, carry):
        for i in range(GROUP):
            code = lists[which, step * GROUP + i]
            at = code % leaves
            rest = code // leaves
            into = rest % leaves
            times = (rest // leaves).astype(jnp.float32)
            square = jnp.maximum(dot(source[at], target[into], NN), TINY)
            distance = square * lax.rsqrt(square)
            high, low = halves((distance + LOG2E) * jnp.exp2(-distance))
            both = split[at]
            total[into] += (dot(both, high, NN) + dot(both, low, NN)) * times
        return carry

    groups = (lists[which + 3, 0] + GROUP - 1) // GROUP
    numerator, parts = part
    start, stop = groups * numerator // parts, groups * (numerator + 1) // parts
    lax.fori_loop(start, stop, group, 0)
    for leaf in range(leaves):
        cut = slice(leaf * size, (leaf + 1) * size)
        value = (total[leaf, :rhs] + total[leaf, rhs:]) * LN2
        out[:, cut] = value if so_far is None else so_far[:, cut] + value


def down_kernel(codes, *refs):
    slots = refs[:-17]
    sources, out = refs[-17:-10], refs[-10]
    table, fields, *held, sems = refs[-9:]
    second, c_two, c_one, c_zero, first, basis = held
    units = slots[0].shape[0]
    targets = [table.at[pl.ds(i * units, units)] for i in range(len(slots))]
    targets += held + [out]
    copies = [
        pltpu.make_async_copy(source, target, sems.at[i])
        for i, (source, target) in enumerate(zip(slots + sources, targets))
    ]
    for copy in copies:
        copy.start()
    for copy in copies[: len(slots) + 2]:
        copy.wait()
    leaves, rank, size = basis.shape
    rhs = out.shape[0]
    lane = lax.broadcasted_iota(jnp.int32, (rhs, 2 * rank), 1)
    partner_count = codes.shape[1]

    def field(node, coupling):
        pieces = []
        for k in range(0, partner_count, 2):
            even, odd = codes[node, k], codes[node, k + 1]
            left = pltpu.roll(table[even // 2], (even % 2) * rank, 1)
            right = pltpu.roll(table[odd // 2], (1 - odd % 2) * rank, 1)
            pieces.append(jnp.where(lane < rank, left, right))
        return product(jnp.concatenate(pieces, axis=1), coupling, NT)

    def level(base, coupling):
        width = min(4, coupling.shape[0] // 2)

        def step(i, carry):
            for j in range(width):
                at = width * i + j
                even = field(2 * (base + at), coupling[2 * at])
                odd = field(2 * (base + at) + 1, coupling[2 * at + 1])
                fields[base + at] = pair_of(even, odd)
            return carry

        lax.fori_loop(0, coupling.shape[0] // (2 * width), step, 0)

    level(leaves // 2 + leaves // 4, c_two)
    copies[len(slots) + 2].wait()
    level(leaves // 2, c_one)
    copies[len(slots) + 3].wait()
    level(0, c_zero)
    for copy in copies[len(slots) + 4 :]:
        copy.wait()

    ones = []
    for p in range(leaves // 4):
        pair = fields[leaves // 2 + leaves // 4 + p // 2]
        top = pair[:, :rank] if p % 2 == 0 else pair[:, rank:]
        ones.append(fields[leaves // 2 + p] + narrow(product(top, second[p], NN)))
    for p in range(leaves // 2):
        pair = ones[p // 2]
        top = pair[:, :rank] if p % 2 == 0 else pair[:, rank:]
        zeros = fields[p] + narrow(product(top, first[p], NN))
        for half in range(2):
            leaf = 2 * p + half
            low = zeros[:, :rank] if half == 0 else zeros[:, rank:]
            cut = slice(leaf * size, (leaf + 1) * size)
            out[:, cut] += narrow(product(low, basis[leaf], NN))


def whole_vmem(n):
    return [pl.BlockSpec(memory_space=pltpu.VMEM)] * n


def params(mebibytes):
    return pltpu.CompilerParams(vmem_limit_bytes=mebibytes * 2**20)


def on_device(
    devices,
    points,
    input_vectors,
    leaf_basis,
    transfer_one,
    transfer_two,
    coupling_zero,
    coupling_one,
    coupling_two,
    neighbour_leaves,
    far_zero,
    far_one,
    far_two,
):
    leaves, rank, size = leaf_basis.shape
    rhs = input_vectors.shape[0]
    tie = lax.optimization_barrier
    before = [(i, i + 1) for i in range(devices - 1)]
    after = [(i + 1, i) for i in range(devices - 1)]
    stacked = pl.pallas_call(
        pack_kernel,
        out_shape=jax.ShapeDtypeStruct((rhs, points.shape[1] + size), jnp.float32),
        in_specs=[pl.BlockSpec(memory_space=pl.ANY), pl.BlockSpec(memory_space=pltpu.VMEM)],
        out_specs=pl.BlockSpec(memory_space=pltpu.VMEM),
        scratch_shapes=[pltpu.SemaphoreType.DMA(())],
        compiler_params=params(8),
        name="pack",
    )(input_vectors, points)
    from_before = lax.ppermute(stacked, "leaf", before)
    from_after = lax.ppermute(stacked, "leaf", after)

    lines = devices // 4

    def swap(value, line_step, row_flip, core_flip):
        pairs = []
        for i in range(devices):
            line, row, core = i // 4, i // 2 % 2, i % 2
            there = ((line + line_step) % lines * 2 + (row ^ row_flip)) * 2 + (core ^ core_flip)
            pairs.append((i, there))
        return lax.ppermute(value, "leaf", pairs)

    units = leaves // 2 + leaves // 4 + leaves // 8
    nodes = leaves + leaves // 2 + leaves // 4
    near_count, far_count = neighbour_leaves.shape[1], far_zero.shape[1]
    coeffs, lists = pl.pallas_call(
        up_kernel,
        out_shape=(
            jax.ShapeDtypeStruct((units, rhs, 2 * rank), jnp.float32),
            jax.ShapeDtypeStruct((6, leaves * near_count), jnp.int32),
        ),
        in_specs=whole_vmem(5) + [pl.BlockSpec(memory_space=pl.ANY)],
        out_specs=tuple(whole_vmem(2)),
        compiler_params=params(12),
        name="up",
    )(neighbour_leaves, input_vectors, leaf_basis, transfer_one, transfer_two, stacked)
    codes = pl.pallas_call(
        functools.partial(pick_kernel, lines, leaves, units),
        out_shape=jax.ShapeDtypeStruct((nodes, far_count), jnp.int32),
        in_specs=whole_vmem(3),
        out_specs=pl.BlockSpec(memory_space=pltpu.VMEM),
        compiler_params=params(2),
        name="picks",
    )(far_zero, far_one, far_two)

    def near_field(which, part, block, work, near, *later):
        operands = (block,) if near is None else (block, near)
        return pl.pallas_call(
            functools.partial(near_kernel, which, part, leaves),
            out_shape=jax.ShapeDtypeStruct(input_vectors.shape, jnp.float32),
            in_specs=[pl.BlockSpec(memory_space=pltpu.SMEM)]
            + whole_vmem(1 + len(operands))
            + [pl.BlockSpec(memory_space=pl.ANY)] * len(later),
            out_specs=pl.BlockSpec(memory_space=pltpu.VMEM),
            scratch_shapes=[
                pltpu.VMEM((leaves, 2 * rhs, size), jnp.bfloat16),
                pltpu.VMEM((leaves, size, 32), jnp.bfloat16),
                pltpu.VMEM((leaves, 32, size), jnp.bfloat16),
                pltpu.VMEM((leaves, 2 * rhs, size), jnp.float32),
            ],
            cost_estimate=pl.CostEstimate(
                flops=work, bytes_accessed=3 * 2**20, transcendentals=0
            ),
            compiler_params=params(NEAR_MEBIBYTES),
            name=("near_before", "near_own", "near_after")[which],
        )(lists, points, *operands, *later)

    far_end = lines - 1
    held = {(0, 0): coeffs}
    for step, towards in {1: 1, far_end: -1}.items():
        held[0, step] = swap(coeffs, towards, 0, 0)
    held[1, 0] = swap(coeffs, 0, 1, 0)
    near = near_field(1, (0, 1), stacked, OWN_WORK, None)
    held, near = tie((held, near))
    middle = (lines + 1) // 2
    for step in range(2, middle + 1):
        if (0, step) not in held:
            held[0, step] = swap(held[0, step - 1], 1, 0, 0)
    for step in range(far_end - 1, middle, -1):
        held[0, step] = swap(held[0, step + 1], -1, 0, 0)
    if far_end > 1:
        held[1, far_end] = swap(held[0, far_end], 0, 1, 0)
    ends = [held[0, step] for step in sorted({1, far_end})]
    near = near_field(0, (0, 1), from_before, NEAR_WORK, near, from_after, *ends)
    along, near = tie(([held[0, step] for step in range(lines)], near))
    for step in range(2, far_end):
        held[1, step] = swap(along[step], 0, 1, 0)
    if (1, 1) not in held:
        behind, _ = tie((held[1, 0], along))
        held[1, 1] = swap(behind, 1, 0, 0)
    early = {(0, step): value for step, value in enumerate(along)}
    early[1, 0], near = tie((held[1, 0], near))
    across = {key: swap(value, 0, 0, 1) for key, value in early.items()}
    near = near_field(2, (0, 1), from_after, NEAR_WORK, near, *along[2:far_end])
    late = {key: value for key, value in held.items() if key not in early}
    late, near = tie((late, near))
    across.update({key: swap(value, 0, 0, 1) for key, value in late.items()})
    order = [(row, step) for row in range(2) for step in range(lines)]
    slots = [{**early, **late}[key] for key in order] + [across[key] for key in order]

    operands = (
        transfer_two,
        coupling_two,
        coupling_one,
        coupling_zero,
        transfer_one,
        leaf_basis,
    )
    copied = len(slots) + len(operands) + 1
    return pl.pallas_call(
        down_kernel,
        out_shape=jax.ShapeDtypeStruct(input_vectors.shape, jnp.float32),
        in_specs=[pl.BlockSpec(memory_space=pltpu.SMEM)]
        + [pl.BlockSpec(memory_space=pl.ANY)] * copied,
        out_specs=pl.BlockSpec(memory_space=pltpu.VMEM),
        scratch_shapes=[
            pltpu.VMEM((devices * units, rhs, 2 * rank), jnp.float32),
            pltpu.VMEM((units, rhs, 2 * rank), jnp.float32),
        ]
        + [pltpu.VMEM(operand.shape, jnp.float32) for operand in operands]
        + [pltpu.SemaphoreType.DMA((copied,))],
        compiler_params=params(DOWN_MEBIBYTES),
        name="down",
    )(codes, *slots, *operands, near)


def solution(mesh):
    whole = ("groups", "leaf")
    columns, nodes, lists = P(None, whole), P(whole, None, None), P(whole, None)
    return jax.shard_map(
        functools.partial(on_device, mesh.shape["leaf"]),
        mesh=mesh,
        in_specs=(columns, columns) + (nodes,) * 6 + (lists,) * 4,
        out_specs=columns,
        check_vma=False,
    )
```

```python
import functools
import math

import jax
import jax.numpy as jnp
from jax import lax
from jax.experimental import pallas as pl
from jax.experimental.pallas import tpu as pltpu
from jax.sharding import PartitionSpec as P

LOG2E = math.log2(math.e)
LN2 = math.log(2.0)
SCALE = math.sqrt(3.0) / 0.05 * LOG2E
TINY = 1e-10
NN = (((1,), (0,)), ((), ()))
NT = (((1,), (1,)), ((), ()))
GROUP = 16
NEAR_WORK = 10**6
OWN_WORK = 10**6
NEAR_MEBIBYTES = 16
DOWN_MEBIBYTES = 56


def halves(value):
    high = value.astype(jnp.bfloat16)
    low = (value - high.astype(jnp.float32)).astype(jnp.bfloat16)
    return high, low


def product(left, right, dims):
    across = 1 if dims == NN else 0
    both = lax.dot_general(
        jnp.concatenate(halves(left), axis=0),
        jnp.concatenate(halves(right), axis=across),
        dims,
        preferred_element_type=jnp.float32,
    )
    rows = left.shape[0]
    return both[:rows] + both[rows:]


def folded(wide):
    return wide + pltpu.roll(wide, wide.shape[1] // 2, 1)


def narrow(wide):
    width = wide.shape[1] // 2
    return wide[:, :width] + wide[:, width:]


def pair_of(even, odd):
    lane = lax.broadcasted_iota(jnp.int32, even.shape, 1)
    return jnp.where(lane < even.shape[1] // 2, folded(even), folded(odd))


def up_kernel(neighbours, vectors, basis, first, second, _, out, lists):
    me = lax.axis_index("leaf")
    leaves, _, size = basis.shape
    pairs = []
    for pair in range(leaves // 2):
        both = []
        for leaf in (2 * pair, 2 * pair + 1):
            columns = vectors[:, leaf * size : (leaf + 1) * size]
            both.append(product(columns, basis[leaf], NT))
        pairs.append(pair_of(*both))
        out[pair] = pairs[pair]
    base = len(pairs)
    for transfer in (first, second):
        nodes = [product(pairs[i], transfer[i], NT) for i in range(len(pairs))]
        pairs = [pair_of(*nodes[2 * i : 2 * i + 2]) for i in range(len(nodes) // 2)]
        for i, pair in enumerate(pairs):
            out[base + i] = pair
        base += len(pairs)
    pair_lists(neighbours[...] - (me - 1) * leaves, leaves, lists)


def pick_kernel(lines, leaves, units, far_zero, far_one, far_two, codes):
    me = lax.axis_index("leaf")
    unit, row = 0, 0
    for far, nodes in ((far_zero, leaves), (far_one, leaves // 2), (far_two, leaves // 4)):
        owner = far[...] // nodes
        local = far[...] % nodes
        step = (me // 4 - owner // 4 + lines) % lines
        across = (me // 2 + owner // 2) % 2
        core = (me + owner) % 2
        slot = (core * 2 + across) * lines + step
        codes[row : row + nodes] = (slot * units + unit + local // 2) * 2 + local % 2
        unit += nodes // 2
        row += nodes


def thirds(value):
    high = value.astype(jnp.bfloat16).astype(jnp.float32)
    rest = value - high
    middle = rest.astype(jnp.bfloat16).astype(jnp.float32)
    low = (rest - middle).astype(jnp.bfloat16).astype(jnp.float32)
    return high, middle, low


def features(points, centre, source):
    scaled = (points - centre) * SCALE
    high, middle, low = thirds(scaled)
    square = jnp.sum(scaled * scaled, axis=0, keepdims=True)
    parts = jnp.concatenate(thirds(square), axis=0)
    ones = jnp.ones_like(parts)
    pad = jnp.zeros((8, points.shape[1]), jnp.float32)
    if source:
        rows = [high, high, middle, middle, high, low, parts, ones, pad]
    else:
        rows = [-2.0 * v for v in (high, middle, high, middle, low, high)]
        rows += [ones, parts, pad]
    return jnp.concatenate(rows, axis=0)


def pair_lists(relative, leaves, out):
    targets, count = relative.shape
    ids = relative.astype(jnp.float32)
    column = lax.broadcasted_iota(jnp.int32, (targets, count), 1)
    row = lax.broadcasted_iota(jnp.int32, (targets, count), 0)
    times = jnp.zeros((targets, count), jnp.float32)
    earlier = jnp.zeros((targets, count), jnp.float32)
    for k in range(count):
        same = jnp.where(ids == ids[:, k : k + 1], 1.0, 0.0)
        times += same
        earlier += jnp.where(column > k, same, 0.0)
    before = jnp.where(
        lax.broadcasted_iota(jnp.int32, (count, count), 0)
        < lax.broadcasted_iota(jnp.int32, (count, count), 1),
        1.0,
        0.0,
    )
    above = jnp.where(
        lax.broadcasted_iota(jnp.int32, (targets, targets), 1)
        < lax.broadcasted_iota(jnp.int32, (targets, targets), 0),
        1.0,
        0.0,
    )
    width = targets * count
    place = lax.broadcasted_iota(jnp.int32, (targets, width), 1).astype(jnp.float32)
    for i in range(3):
        source = relative - i * leaves
        keep = jnp.where((source >= 0) & (source < leaves) & (earlier == 0.0), 1.0, 0.0)
        rank = lax.dot_general(keep, before, NN, preferred_element_type=jnp.float32)
        sums = jnp.sum(keep, axis=1, keepdims=True)
        wide = jnp.broadcast_to(sums, (targets, count))
        rank += lax.dot_general(above, wide, NN, preferred_element_type=jnp.float32)
        code = (times * targets + row.astype(jnp.float32)) * leaves
        code = (code + source.astype(jnp.float32)) * keep
        rank = jnp.where(keep > 0.0, rank, -1.0)
        flat = jnp.zeros((targets, width), jnp.float32)
        for k in range(count):
            flat += jnp.where(rank[:, k : k + 1] == place, code[:, k : k + 1], 0.0)
        out[i : i + 1] = jnp.sum(flat, axis=0, keepdims=True).astype(jnp.int32)
        total = jnp.sum(sums, axis=0, keepdims=True)
        out[i + 3 : i + 4] = jnp.broadcast_to(total, (1, width)).astype(jnp.int32)


def pack_kernel(vectors, points, out, sem):
    width = vectors.shape[1]
    copy = pltpu.make_async_copy(vectors, out.at[:, pl.ds(0, width)], sem)
    copy.start()
    size = out.shape[1] - width
    out[:, width:] = jnp.zeros((out.shape[0], size), jnp.float32)
    for leaf in range(width // size):
        cut = slice(leaf * size, (leaf + 1) * size)
        out[4 * leaf : 4 * leaf + 3, width:] = points[:, cut]
    copy.wait()


def near_kernel(which, part, leaves, lists, p_own, block, *refs):
    so_far = None if which == 1 else refs[0]
    out, split, source, target, total = refs[-5:]
    rhs, size = split.shape[1] // 2, split.shape[2]
    own = p_own[...]
    top = jnp.max(own, axis=1, keepdims=True)
    bottom = jnp.min(own, axis=1, keepdims=True)
    centre = 0.5 * (top + bottom)
    wide = features(own, centre, False).astype(jnp.bfloat16)
    wide_points = [block[4 * leaf : 4 * leaf + 3, leaves * size :] for leaf in range(leaves)]
    there = features(jnp.concatenate(wide_points, axis=1), centre, True)
    for leaf in range(leaves):
        cut = slice(leaf * size, (leaf + 1) * size)
        target[leaf] = wide[:, cut]
        total[leaf] = jnp.zeros(total.shape[1:], jnp.float32)
        source[leaf] = there[:, cut].T.astype(jnp.bfloat16)
        high, low = halves(block[:rhs, cut])
        split[leaf, :rhs] = high
        split[leaf, rhs:] = low

    dot = functools.partial(lax.dot_general, preferred_element_type=jnp.float32)

    def group(step, carry):
        for i in range(GROUP):
            code = lists[which, step * GROUP + i]
            at = code % leaves
            rest = code // leaves
            into = rest % leaves
            times = (rest // leaves).astype(jnp.float32)
            square = jnp.maximum(dot(source[at], target[into], NN), TINY)
            distance = square * lax.rsqrt(square)
            high, low = halves((distance + LOG2E) * jnp.exp2(-distance))
            both = split[at]
            total[into] += (dot(both, high, NN) + dot(both, low, NN)) * times
        return carry

    groups = (lists[which + 3, 0] + GROUP - 1) // GROUP
    numerator, parts = part
    start, stop = groups * numerator // parts, groups * (numerator + 1) // parts
    lax.fori_loop(start, stop, group, 0)
    for leaf in range(leaves):
        cut = slice(leaf * size, (leaf + 1) * size)
        value = (total[leaf, :rhs] + total[leaf, rhs:]) * LN2
        out[:, cut] = value if so_far is None else so_far[:, cut] + value


def down_kernel(codes, *refs):
    slots = refs[:-17]
    sources, out = refs[-17:-10], refs[-10]
    table, fields, *held, sems = refs[-9:]
    second, c_two, c_one, c_zero, first, basis = held
    units = slots[0].shape[0]
    targets = [table.at[pl.ds(i * units, units)] for i in range(len(slots))]
    targets += held + [out]
    copies = [
        pltpu.make_async_copy(source, target, sems.at[i])
        for i, (source, target) in enumerate(zip(slots + sources, targets))
    ]
    for copy in copies:
        copy.start()
    for copy in copies[: len(slots) + 2]:
        copy.wait()
    leaves, rank, size = basis.shape
    rhs = out.shape[0]
    lane = lax.broadcasted_iota(jnp.int32, (rhs, 2 * rank), 1)
    partner_count = codes.shape[1]

    def field(node, coupling):
        pieces = []
        for k in range(0, partner_count, 2):
            even, odd = codes[node, k], codes[node, k + 1]
            left, right = table[even // 2], table[odd // 2]
            straight = jnp.where(lane < rank, left, right)
            turned = pltpu.roll(jnp.where(lane < rank, right, left), rank, 1)
            other = jnp.where(lane < rank, even % 2, 1 - odd % 2)
            pieces.append(jnp.where(other == 0, straight, turned))
        return product(jnp.concatenate(pieces, axis=1), coupling, NT)

    def level(base, coupling):
        width = min(8, coupling.shape[0] // 2)

        def step(i, carry):
            for j in range(width):
                at = width * i + j
                even = field(2 * (base + at), coupling[2 * at])
                odd = field(2 * (base + at) + 1, coupling[2 * at + 1])
                fields[base + at] = pair_of(even, odd)
            return carry

        lax.fori_loop(0, coupling.shape[0] // (2 * width), step, 0)

    level(leaves // 2 + leaves // 4, c_two)
    copies[len(slots) + 2].wait()
    level(leaves // 2, c_one)
    copies[len(slots) + 3].wait()
    level(0, c_zero)
    for copy in copies[len(slots) + 4 :]:
        copy.wait()

    ones = []
    for p in range(leaves // 4):
        pair = fields[leaves // 2 + leaves // 4 + p // 2]
        top = pair[:, :rank] if p % 2 == 0 else pair[:, rank:]
        ones.append(fields[leaves // 2 + p] + narrow(product(top, second[p], NN)))
    for p in range(leaves // 2):
        pair = ones[p // 2]
        top = pair[:, :rank] if p % 2 == 0 else pair[:, rank:]
        zeros = fields[p] + narrow(product(top, first[p], NN))
        for half in range(2):
            leaf = 2 * p + half
            low = zeros[:, :rank] if half == 0 else zeros[:, rank:]
            cut = slice(leaf * size, (leaf + 1) * size)
            out[:, cut] += narrow(product(low, basis[leaf], NN))


def whole_vmem(n):
    return [pl.BlockSpec(memory_space=pltpu.VMEM)] * n


def params(mebibytes):
    return pltpu.CompilerParams(vmem_limit_bytes=mebibytes * 2**20)


def on_device(
    devices,
    points,
    input_vectors,
    leaf_basis,
    transfer_one,
    transfer_two,
    coupling_zero,
    coupling_one,
    coupling_two,
    neighbour_leaves,
    far_zero,
    far_one,
    far_two,
):
    leaves, rank, size = leaf_basis.shape
    rhs = input_vectors.shape[0]
    tie = lax.optimization_barrier
    before = [(i, i + 1) for i in range(devices - 1)]
    after = [(i + 1, i) for i in range(devices - 1)]
    stacked = pl.pallas_call(
        pack_kernel,
        out_shape=jax.ShapeDtypeStruct((rhs, points.shape[1] + size), jnp.float32),
        in_specs=[pl.BlockSpec(memory_space=pl.ANY), pl.BlockSpec(memory_space=pltpu.VMEM)],
        out_specs=pl.BlockSpec(memory_space=pltpu.VMEM),
        scratch_shapes=[pltpu.SemaphoreType.DMA(())],
        compiler_params=params(8),
        name="pack",
    )(input_vectors, points)
    from_before = lax.ppermute(stacked, "leaf", before)
    from_after = lax.ppermute(stacked, "leaf", after)

    lines = devices // 4

    def swap(value, line_step, row_flip, core_flip):
        pairs = []
        for i in range(devices):
            line, row, core = i // 4, i // 2 % 2, i % 2
            there = ((line + line_step) % lines * 2 + (row ^ row_flip)) * 2 + (core ^ core_flip)
            pairs.append((i, there))
        return lax.ppermute(value, "leaf", pairs)

    units = leaves // 2 + leaves // 4 + leaves // 8
    nodes = leaves + leaves // 2 + leaves // 4
    near_count, far_count = neighbour_leaves.shape[1], far_zero.shape[1]
    coeffs, lists = pl.pallas_call(
        up_kernel,
        out_shape=(
            jax.ShapeDtypeStruct((units, rhs, 2 * rank), jnp.float32),
            jax.ShapeDtypeStruct((6, leaves * near_count), jnp.int32),
        ),
        in_specs=whole_vmem(5) + [pl.BlockSpec(memory_space=pl.ANY)],
        out_specs=tuple(whole_vmem(2)),
        compiler_params=params(12),
        name="up",
    )(neighbour_leaves, input_vectors, leaf_basis, transfer_one, transfer_two, stacked)
    codes = pl.pallas_call(
        functools.partial(pick_kernel, lines, leaves, units),
        out_shape=jax.ShapeDtypeStruct((nodes, far_count), jnp.int32),
        in_specs=whole_vmem(3),
        out_specs=pl.BlockSpec(memory_space=pltpu.VMEM),
        compiler_params=params(2),
        name="picks",
    )(far_zero, far_one, far_two)

    def near_field(which, part, block, work, near, *later):
        operands = (block,) if near is None else (block, near)
        return pl.pallas_call(
            functools.partial(near_kernel, which, part, leaves),
            out_shape=jax.ShapeDtypeStruct(input_vectors.shape, jnp.float32),
            in_specs=[pl.BlockSpec(memory_space=pltpu.SMEM)]
            + whole_vmem(1 + len(operands))
            + [pl.BlockSpec(memory_space=pl.ANY)] * len(later),
            out_specs=pl.BlockSpec(memory_space=pltpu.VMEM),
            scratch_shapes=[
                pltpu.VMEM((leaves, 2 * rhs, size), jnp.bfloat16),
                pltpu.VMEM((leaves, size, 32), jnp.bfloat16),
                pltpu.VMEM((leaves, 32, size), jnp.bfloat16),
                pltpu.VMEM((leaves, 2 * rhs, size), jnp.float32),
            ],
            cost_estimate=pl.CostEstimate(
                flops=work, bytes_accessed=3 * 2**20, transcendentals=0
            ),
            compiler_params=params(NEAR_MEBIBYTES),
            name=("near_before", "near_own", "near_after")[which],
        )(lists, points, *operands, *later)

    far_end = lines - 1
    held = {(0, 0): coeffs}
    for step, towards in {1: 1, far_end: -1}.items():
        held[0, step] = swap(coeffs, towards, 0, 0)
    held[1, 0] = swap(coeffs, 0, 1, 0)
    near = near_field(1, (0, 1), stacked, OWN_WORK, None)
    held, near = tie((held, near))
    middle = (lines + 1) // 2
    for step in range(2, middle + 1):
        if (0, step) not in held:
            held[0, step] = swap(held[0, step - 1], 1, 0, 0)
    for step in range(far_end - 1, middle, -1):
        held[0, step] = swap(held[0, step + 1], -1, 0, 0)
    if far_end > 1:
        held[1, far_end] = swap(held[0, far_end], 0, 1, 0)
    ends = [held[0, step] for step in sorted({1, far_end})]
    near = near_field(0, (0, 1), from_before, NEAR_WORK, near, from_after, *ends)
    along, near = tie(([held[0, step] for step in range(lines)], near))
    for step in range(2, far_end):
        held[1, step] = swap(along[step], 0, 1, 0)
    if (1, 1) not in held:
        behind, _ = tie((held[1, 0], along))
        held[1, 1] = swap(behind, 1, 0, 0)
    early = {(0, step): value for step, value in enumerate(along)}
    early[1, 0], near = tie((held[1, 0], near))
    across = {key: swap(value, 0, 0, 1) for key, value in early.items()}
    near = near_field(2, (0, 1), from_after, NEAR_WORK, near, *along[2:far_end])
    late = {key: value for key, value in held.items() if key not in early}
    late, near = tie((late, near))
    across.update({key: swap(value, 0, 0, 1) for key, value in late.items()})
    order = [(row, step) for row in range(2) for step in range(lines)]
    slots = [{**early, **late}[key] for key in order] + [across[key] for key in order]

    operands = (
        transfer_two,
        coupling_two,
        coupling_one,
        coupling_zero,
        transfer_one,
        leaf_basis,
    )
    copied = len(slots) + len(operands) + 1
    return pl.pallas_call(
        down_kernel,
        out_shape=jax.ShapeDtypeStruct(input_vectors.shape, jnp.float32),
        in_specs=[pl.BlockSpec(memory_space=pltpu.SMEM)]
        + [pl.BlockSpec(memory_space=pl.ANY)] * copied,
        out_specs=pl.BlockSpec(memory_space=pltpu.VMEM),
        scratch_shapes=[
            pltpu.VMEM((devices * units, rhs, 2 * rank), jnp.float32),
            pltpu.VMEM((units, rhs, 2 * rank), jnp.float32),
        ]
        + [pltpu.VMEM(operand.shape, jnp.float32) for operand in operands]
        + [pltpu.SemaphoreType.DMA((copied,))],
        compiler_params=params(DOWN_MEBIBYTES),
        name="down",
    )(codes, *slots, *operands, near)


def solution(mesh):
    whole = ("groups", "leaf")
    columns, nodes, lists = P(None, whole), P(whole, None, None), P(whole, None)
    return jax.shard_map(
        functools.partial(on_device, mesh.shape["leaf"]),
        mesh=mesh,
        in_specs=(columns, columns) + (nodes,) * 6 + (lists,) * 4,
        out_specs=columns,
        check_vma=False,
    )
```

```python
import functools
import math

import jax
import jax.numpy as jnp
from jax import lax
from jax.experimental import pallas as pl
from jax.experimental.pallas import tpu as pltpu
from jax.sharding import PartitionSpec as P

LOG2E = math.log2(math.e)
LN2 = math.log(2.0)
SCALE = math.sqrt(3.0) / 0.05 * LOG2E
TINY = 1e-10
NN = (((1,), (0,)), ((), ()))
NT = (((1,), (1,)), ((), ()))
GROUP = 16
NEAR_WORK = 10**6
OWN_WORK = 10**6
NEAR_MEBIBYTES = 16
DOWN_MEBIBYTES = 56


def halves(value):
    high = value.astype(jnp.bfloat16)
    low = (value - high.astype(jnp.float32)).astype(jnp.bfloat16)
    return high, low


def product(left, right, dims):
    across = 1 if dims == NN else 0
    both = lax.dot_general(
        jnp.concatenate(halves(left), axis=0),
        jnp.concatenate(halves(right), axis=across),
        dims,
        preferred_element_type=jnp.float32,
    )
    rows = left.shape[0]
    return both[:rows] + both[rows:]


def folded(wide):
    return wide + pltpu.roll(wide, wide.shape[1] // 2, 1)


def narrow(wide):
    width = wide.shape[1] // 2
    return wide[:, :width] + wide[:, width:]


def pair_of(even, odd):
    lane = lax.broadcasted_iota(jnp.int32, even.shape, 1)
    return jnp.where(lane < even.shape[1] // 2, folded(even), folded(odd))


def up_kernel(neighbours, vectors, basis, first, second, _, out, lists):
    me = lax.axis_index("leaf")
    leaves, _, size = basis.shape
    pairs = []
    for pair in range(leaves // 2):
        both = []
        for leaf in (2 * pair, 2 * pair + 1):
            columns = vectors[:, leaf * size : (leaf + 1) * size]
            both.append(product(columns, basis[leaf], NT))
        pairs.append(pair_of(*both))
        out[pair] = pairs[pair]
    base = len(pairs)
    for transfer in (first, second):
        nodes = [product(pairs[i], transfer[i], NT) for i in range(len(pairs))]
        pairs = [pair_of(*nodes[2 * i : 2 * i + 2]) for i in range(len(nodes) // 2)]
        for i, pair in enumerate(pairs):
            out[base + i] = pair
        base += len(pairs)
    pair_lists(neighbours[...] - (me - 1) * leaves, leaves, lists)


def pick_kernel(lines, leaves, units, far_zero, far_one, far_two, codes):
    me = lax.axis_index("leaf")
    unit, row = 0, 0
    for far, nodes in ((far_zero, leaves), (far_one, leaves // 2), (far_two, leaves // 4)):
        owner = far[...] // nodes
        local = far[...] % nodes
        step = (me // 4 - owner // 4 + lines) % lines
        across = (me // 2 + owner // 2) % 2
        core = (me + owner) % 2
        slot = (core * 2 + across) * lines + step
        codes[row : row + nodes] = (slot * units + unit + local // 2) * 2 + local % 2
        unit += nodes // 2
        row += nodes


def thirds(value):
    high = value.astype(jnp.bfloat16).astype(jnp.float32)
    rest = value - high
    middle = rest.astype(jnp.bfloat16).astype(jnp.float32)
    low = (rest - middle).astype(jnp.bfloat16).astype(jnp.float32)
    return high, middle, low


def features(points, centre, source):
    scaled = (points - centre) * SCALE
    high, middle, low = thirds(scaled)
    square = jnp.sum(scaled * scaled, axis=0, keepdims=True)
    parts = jnp.concatenate(thirds(square), axis=0)
    ones = jnp.ones_like(parts)
    pad = jnp.zeros((8, points.shape[1]), jnp.float32)
    if source:
        rows = [high, high, middle, middle, high, low, parts, ones, pad]
    else:
        rows = [-2.0 * v for v in (high, middle, high, middle, low, high)]
        rows += [ones, parts, pad]
    return jnp.concatenate(rows, axis=0)


def pair_lists(relative, leaves, out):
    targets, count = relative.shape
    ids = relative.astype(jnp.float32)
    column = lax.broadcasted_iota(jnp.int32, (targets, count), 1)
    row = lax.broadcasted_iota(jnp.int32, (targets, count), 0)
    times = jnp.zeros((targets, count), jnp.float32)
    earlier = jnp.zeros((targets, count), jnp.float32)
    for k in range(count):
        same = jnp.where(ids == ids[:, k : k + 1], 1.0, 0.0)
        times += same
        earlier += jnp.where(column > k, same, 0.0)
    before = jnp.where(
        lax.broadcasted_iota(jnp.int32, (count, count), 0)
        < lax.broadcasted_iota(jnp.int32, (count, count), 1),
        1.0,
        0.0,
    )
    above = jnp.where(
        lax.broadcasted_iota(jnp.int32, (targets, targets), 1)
        < lax.broadcasted_iota(jnp.int32, (targets, targets), 0),
        1.0,
        0.0,
    )
    width = targets * count
    place = lax.broadcasted_iota(jnp.int32, (targets, width), 1).astype(jnp.float32)
    for i in range(3):
        source = relative - i * leaves
        keep = jnp.where((source >= 0) & (source < leaves) & (earlier == 0.0), 1.0, 0.0)
        rank = lax.dot_general(keep, before, NN, preferred_element_type=jnp.float32)
        sums = jnp.sum(keep, axis=1, keepdims=True)
        wide = jnp.broadcast_to(sums, (targets, count))
        rank += lax.dot_general(above, wide, NN, preferred_element_type=jnp.float32)
        code = (times * targets + row.astype(jnp.float32)) * leaves
        code = (code + source.astype(jnp.float32)) * keep
        rank = jnp.where(keep > 0.0, rank, -1.0)
        flat = jnp.zeros((targets, width), jnp.float32)
        for k in range(count):
            flat += jnp.where(rank[:, k : k + 1] == place, code[:, k : k + 1], 0.0)
        out[i : i + 1] = jnp.sum(flat, axis=0, keepdims=True).astype(jnp.int32)
        total = jnp.sum(sums, axis=0, keepdims=True)
        out[i + 3 : i + 4] = jnp.broadcast_to(total, (1, width)).astype(jnp.int32)


def pack_kernel(vectors, points, out, sem):
    width = vectors.shape[1]
    copy = pltpu.make_async_copy(vectors, out.at[:, pl.ds(0, width)], sem)
    copy.start()
    size = out.shape[1] - width
    out[:, width:] = jnp.zeros((out.shape[0], size), jnp.float32)
    for leaf in range(width // size):
        cut = slice(leaf * size, (leaf + 1) * size)
        out[4 * leaf : 4 * leaf + 3, width:] = points[:, cut]
    copy.wait()


def near_kernel(which, part, leaves, lists, p_own, block, *refs):
    so_far = None if which == 1 else refs[0]
    out, split, source, target, total = refs[-5:]
    rhs, size = split.shape[1] // 2, split.shape[2]
    own = p_own[...]
    top = jnp.max(own, axis=1, keepdims=True)
    bottom = jnp.min(own, axis=1, keepdims=True)
    centre = 0.5 * (top + bottom)
    wide = features(own, centre, False).astype(jnp.bfloat16)
    wide_points = [block[4 * leaf : 4 * leaf + 3, leaves * size :] for leaf in range(leaves)]
    there = features(jnp.concatenate(wide_points, axis=1), centre, True)
    for leaf in range(leaves):
        cut = slice(leaf * size, (leaf + 1) * size)
        target[leaf] = wide[:, cut]
        total[leaf] = jnp.zeros(total.shape[1:], jnp.float32)
        source[leaf] = there[:, cut].T.astype(jnp.bfloat16)
        high, low = halves(block[:rhs, cut])
        split[leaf, :rhs] = high
        split[leaf, rhs:] = low

    dot = functools.partial(lax.dot_general, preferred_element_type=jnp.float32)

    def group(step, carry):
        for i in range(GROUP):
            code = lists[which, step * GROUP + i]
            at = code % leaves
            rest = code // leaves
            into = rest % leaves
            times = (rest // leaves).astype(jnp.float32)
            square = jnp.maximum(dot(source[at], target[into], NN), TINY)
            distance = square * lax.rsqrt(square)
            high, low = halves((distance + LOG2E) * jnp.exp2(-distance))
            both = split[at]
            total[into] += (dot(both, high, NN) + dot(both, low, NN)) * times
        return carry

    groups = (lists[which + 3, 0] + GROUP - 1) // GROUP
    numerator, parts = part
    start, stop = groups * numerator // parts, groups * (numerator + 1) // parts
    lax.fori_loop(start, stop, group, 0)
    for leaf in range(leaves):
        cut = slice(leaf * size, (leaf + 1) * size)
        value = (total[leaf, :rhs] + total[leaf, rhs:]) * LN2
        out[:, cut] = value if so_far is None else so_far[:, cut] + value


def down_kernel(codes, *refs):
    slots = refs[:-18]
    sources, out = refs[-18:-11], refs[-11]
    table, fields, *held, total, sems = refs[-10:]
    second, c_two, c_one, c_zero, first, basis = held
    units = slots[0].shape[0]
    targets = [table.at[pl.ds(i * units, units)] for i in range(len(slots))]
    targets += held + [total]
    copies = [
        pltpu.make_async_copy(source, target, sems.at[i])
        for i, (source, target) in enumerate(zip(slots + sources, targets))
    ]
    for copy in copies:
        copy.start()
    for copy in copies[: len(slots) + 2]:
        copy.wait()
    leaves, rank, size = basis.shape
    rhs = out.shape[0]
    lane = lax.broadcasted_iota(jnp.int32, (rhs, 2 * rank), 1)
    partner_count = codes.shape[1]

    def field(node, coupling):
        pieces = []
        for k in range(0, partner_count, 2):
            even, odd = codes[node, k], codes[node, k + 1]
            left, right = table[even // 2], table[odd // 2]
            straight = jnp.where(lane < rank, left, right)
            turned = pltpu.roll(jnp.where(lane < rank, right, left), rank, 1)
            other = jnp.where(lane < rank, even % 2, 1 - odd % 2)
            pieces.append(jnp.where(other == 0, straight, turned))
        return product(jnp.concatenate(pieces, axis=1), coupling, NT)

    def level(base, coupling):
        width = min(8, coupling.shape[0] // 2)

        def step(i, carry):
            for j in range(width):
                at = width * i + j
                even = field(2 * (base + at), coupling[2 * at])
                odd = field(2 * (base + at) + 1, coupling[2 * at + 1])
                fields[base + at] = pair_of(even, odd)
            return carry

        lax.fori_loop(0, coupling.shape[0] // (2 * width), step, 0)

    level(leaves // 2 + leaves // 4, c_two)
    copies[len(slots) + 2].wait()
    level(leaves // 2, c_one)
    copies[len(slots) + 3].wait()
    level(0, c_zero)
    for copy in copies[len(slots) + 4 :]:
        copy.wait()

    ones, results = [], []
    for p in range(leaves // 4):
        pair = fields[leaves // 2 + leaves // 4 + p // 2]
        top = pair[:, :rank] if p % 2 == 0 else pair[:, rank:]
        ones.append(fields[leaves // 2 + p] + narrow(product(top, second[p], NN)))
    for p in range(leaves // 2):
        pair = ones[p // 2]
        top = pair[:, :rank] if p % 2 == 0 else pair[:, rank:]
        zeros = fields[p] + narrow(product(top, first[p], NN))
        for half in range(2):
            leaf = 2 * p + half
            low = zeros[:, :rank] if half == 0 else zeros[:, rank:]
            cut = slice(leaf * size, (leaf + 1) * size)
            total[:, cut] += narrow(product(low, basis[leaf], NN))
        done = pl.ds(2 * p * size, 2 * size)
        there = pltpu.make_async_copy(total.at[:, done], out.at[:, done], sems.at[p])
        there.start()
        results.append(there)
    for there in results:
        there.wait()


def whole_vmem(n):
    return [pl.BlockSpec(memory_space=pltpu.VMEM)] * n


def params(mebibytes):
    return pltpu.CompilerParams(vmem_limit_bytes=mebibytes * 2**20)


def on_device(
    devices,
    points,
    input_vectors,
    leaf_basis,
    transfer_one,
    transfer_two,
    coupling_zero,
    coupling_one,
    coupling_two,
    neighbour_leaves,
    far_zero,
    far_one,
    far_two,
):
    leaves, rank, size = leaf_basis.shape
    rhs = input_vectors.shape[0]
    tie = lax.optimization_barrier
    before = [(i, i + 1) for i in range(devices - 1)]
    after = [(i + 1, i) for i in range(devices - 1)]
    stacked = pl.pallas_call(
        pack_kernel,
        out_shape=jax.ShapeDtypeStruct((rhs, points.shape[1] + size), jnp.float32),
        in_specs=[pl.BlockSpec(memory_space=pl.ANY), pl.BlockSpec(memory_space=pltpu.VMEM)],
        out_specs=pl.BlockSpec(memory_space=pltpu.VMEM),
        scratch_shapes=[pltpu.SemaphoreType.DMA(())],
        compiler_params=params(8),
        name="pack",
    )(input_vectors, points)
    from_before = lax.ppermute(stacked, "leaf", before)
    from_after = lax.ppermute(stacked, "leaf", after)

    lines = devices // 4

    def swap(value, line_step, row_flip, core_flip):
        pairs = []
        for i in range(devices):
            line, row, core = i // 4, i // 2 % 2, i % 2
            there = ((line + line_step) % lines * 2 + (row ^ row_flip)) * 2 + (core ^ core_flip)
            pairs.append((i, there))
        return lax.ppermute(value, "leaf", pairs)

    units = leaves // 2 + leaves // 4 + leaves // 8
    nodes = leaves + leaves // 2 + leaves // 4
    near_count, far_count = neighbour_leaves.shape[1], far_zero.shape[1]
    coeffs, lists = pl.pallas_call(
        up_kernel,
        out_shape=(
            jax.ShapeDtypeStruct((units, rhs, 2 * rank), jnp.float32),
            jax.ShapeDtypeStruct((6, leaves * near_count), jnp.int32),
        ),
        in_specs=whole_vmem(5) + [pl.BlockSpec(memory_space=pl.ANY)],
        out_specs=tuple(whole_vmem(2)),
        compiler_params=params(12),
        name="up",
    )(neighbour_leaves, input_vectors, leaf_basis, transfer_one, transfer_two, stacked)
    codes = pl.pallas_call(
        functools.partial(pick_kernel, lines, leaves, units),
        out_shape=jax.ShapeDtypeStruct((nodes, far_count), jnp.int32),
        in_specs=whole_vmem(3),
        out_specs=pl.BlockSpec(memory_space=pltpu.VMEM),
        compiler_params=params(2),
        name="picks",
    )(far_zero, far_one, far_two)

    def near_field(which, part, block, work, near, *later):
        operands = (block,) if near is None else (block, near)
        return pl.pallas_call(
            functools.partial(near_kernel, which, part, leaves),
            out_shape=jax.ShapeDtypeStruct(input_vectors.shape, jnp.float32),
            in_specs=[pl.BlockSpec(memory_space=pltpu.SMEM)]
            + whole_vmem(1 + len(operands))
            + [pl.BlockSpec(memory_space=pl.ANY)] * len(later),
            out_specs=pl.BlockSpec(memory_space=pltpu.VMEM),
            scratch_shapes=[
                pltpu.VMEM((leaves, 2 * rhs, size), jnp.bfloat16),
                pltpu.VMEM((leaves, size, 32), jnp.bfloat16),
                pltpu.VMEM((leaves, 32, size), jnp.bfloat16),
                pltpu.VMEM((leaves, 2 * rhs, size), jnp.float32),
            ],
            cost_estimate=pl.CostEstimate(
                flops=work, bytes_accessed=3 * 2**20, transcendentals=0
            ),
            compiler_params=params(NEAR_MEBIBYTES),
            name=("near_before", "near_own", "near_after")[which],
        )(lists, points, *operands, *later)

    far_end = lines - 1
    held = {(0, 0): coeffs}
    for step, towards in {1: 1, far_end: -1}.items():
        held[0, step] = swap(coeffs, towards, 0, 0)
    held[1, 0] = swap(coeffs, 0, 1, 0)
    near = near_field(1, (0, 1), stacked, OWN_WORK, None)
    held, near = tie((held, near))
    middle = (lines + 1) // 2
    for step in range(2, middle + 1):
        if (0, step) not in held:
            held[0, step] = swap(held[0, step - 1], 1, 0, 0)
    for step in range(far_end - 1, middle, -1):
        held[0, step] = swap(held[0, step + 1], -1, 0, 0)
    if far_end > 1:
        held[1, far_end] = swap(held[0, far_end], 0, 1, 0)
    ends = [held[0, step] for step in sorted({1, far_end})]
    near = near_field(0, (0, 1), from_before, NEAR_WORK, near, from_after, *ends)
    along, near = tie(([held[0, step] for step in range(lines)], near))
    for step in range(2, far_end):
        held[1, step] = swap(along[step], 0, 1, 0)
    if (1, 1) not in held:
        behind, _ = tie((held[1, 0], along))
        held[1, 1] = swap(behind, 1, 0, 0)
    early = {(0, step): value for step, value in enumerate(along)}
    early[1, 0], near = tie((held[1, 0], near))
    across = {key: swap(value, 0, 0, 1) for key, value in early.items()}
    near = near_field(2, (0, 1), from_after, NEAR_WORK, near, *along[2:far_end])
    late = {key: value for key, value in held.items() if key not in early}
    late, near = tie((late, near))
    across.update({key: swap(value, 0, 0, 1) for key, value in late.items()})
    order = [(row, step) for row in range(2) for step in range(lines)]
    slots = [{**early, **late}[key] for key in order] + [across[key] for key in order]

    operands = (
        transfer_two,
        coupling_two,
        coupling_one,
        coupling_zero,
        transfer_one,
        leaf_basis,
    )
    copied = len(slots) + len(operands) + 1
    return pl.pallas_call(
        down_kernel,
        out_shape=jax.ShapeDtypeStruct(input_vectors.shape, jnp.float32),
        in_specs=[pl.BlockSpec(memory_space=pltpu.SMEM)]
        + [pl.BlockSpec(memory_space=pl.ANY)] * copied,
        out_specs=pl.BlockSpec(memory_space=pl.ANY),
        scratch_shapes=[
            pltpu.VMEM((devices * units, rhs, 2 * rank), jnp.float32),
            pltpu.VMEM((units, rhs, 2 * rank), jnp.float32),
        ]
        + [pltpu.VMEM(operand.shape, jnp.float32) for operand in operands]
        + [pltpu.VMEM(near.shape, jnp.float32), pltpu.SemaphoreType.DMA((copied,))],
        compiler_params=params(DOWN_MEBIBYTES),
        name="down",
    )(codes, *slots, *operands, near)


def solution(mesh):
    whole = ("groups", "leaf")
    columns, nodes, lists = P(None, whole), P(whole, None, None), P(whole, None)
    return jax.shard_map(
        functools.partial(on_device, mesh.shape["leaf"]),
        mesh=mesh,
        in_specs=(columns, columns) + (nodes,) * 6 + (lists,) * 4,
        out_specs=columns,
        check_vma=False,
    )
```
